512 devices in a mesh: gx: 32 (over z_hi, x, core), gy: 16 (over y, z_lo).
Axes of the slice: x: 4, y: 4, z: 16 (z_hi: 4, z_lo: 4; z = z_hi * 4 + z_lo), core: 2. Of those that a mesh axis runs over, the one named last changes fastest.
Arguments:
- fields: float32 [8, 512, 512, 128], P(None, 'gx', 'gy'), may hold values from -12 to 12
- displacement: float32 [2, 512, 512], P(None, 'gx', 'gy'), may hold values from -0.3 to 0.3
- donor_tile: int32 [512, 512, 4], P('gx', 'gy'), may hold values from 0 to 31, as said below
- donor_offset: int32 [512, 512, 4], P('gx', 'gy'), may hold values from 0 to 511, as said below
- donor_count: int32 [512, 512], P('gx', 'gy'), may hold values from 1 to 4
Outputs:
- moved_mesh: float32 [2, 512, 512], P(None, 'gx', 'gy')
- remapped: float32 [8, 512, 512, 128], P(None, 'gx', 'gy')
The draws below stay inside these ranges and needn't reach their ends.
Inputs may be any that keep to these rules, and one draw needn't show every extreme that they name: `donor_tile`: the owning tile lies within one of the new column's own gx index; only slot 0 of a column may name another tile, and of the columns of one tile at most 32 name each neighbouring tile in slot 0, a number reached in every draw. `donor_offset`: the donor lies in the same gy tile as the new column.
All inputs are finite; a program needn't handle non-finite values.
Results may differ from the reference program's by a relative error of at most 0.0001.
Values sent between devices are 32-bit elements; how exact they have to be, the bound alone decides.
No kernel may reach another device: no remote copies, remote signals or barrier semaphores. Data moves between devices by JAX's collectives and lax.ppermute only.
A program may use at most 64 MiB of HBM per device.

```python
import math
import jax
import jax.numpy as jnp
from jax import lax

CX = 16
CY = 32
NZ = 128
FIELDS = 8
DONORS = 4
CAP = 32
SWEEPS = 3
STEPS = 2
NX = 512
NY = 512


def donor_plan(key):
    tiles_x = NX // CX
    tiles_y = NY // CY
    tile_cells = CX * CY
    key_loads, key_scores, key_places = jax.random.split(key, 3)
    drawn = jax.random.randint(key_loads, (2, tiles_x, tiles_y), CAP // 3, CAP + 1)
    forced = (jnp.arange(tiles_y) == 0)[None, None, :]
    loads = jnp.where(forced, CAP, drawn)
    tile_ids = jnp.arange(tiles_x, dtype=jnp.int32)[:, None]
    left_load = jnp.where(tile_ids > 0, loads[0], 0)
    right_load = jnp.where(tile_ids < tiles_x - 1, loads[1], 0)
    scores = jax.random.randint(key_scores, (tiles_x, tiles_y, tile_cells), 0, 1 << 20) * tile_cells + jnp.arange(tile_cells, dtype=jnp.int32)
    rank_order = jnp.argsort(jnp.argsort(scores, axis=-1), axis=-1)
    towards = jnp.where(rank_order < left_load[:, :, None], -1, jnp.where(rank_order < (left_load + right_load)[:, :, None], 1, 0))
    first_owner = tile_ids[:, :, None] + towards
    rest_owner = jnp.broadcast_to(tile_ids[:, :, None, None], (tiles_x, tiles_y, tile_cells, DONORS - 1))
    owners = jnp.concatenate([first_owner[..., None], rest_owner], axis=-1)
    places = jax.random.randint(key_places, (tiles_x, tiles_y, tile_cells, DONORS), 0, tile_cells)
    return (arrange_tiles(owners, tiles_x, tiles_y), arrange_tiles(places, tiles_x, tiles_y))


def arrange_tiles(values, tiles_x, tiles_y):
    shaped = values.reshape(tiles_x, tiles_y, CX, CY, DONORS).transpose(0, 2, 1, 3, 4)
    return shaped.reshape(NX, NY, DONORS).astype(jnp.int32)


def draw_donor_tile(key, part):
    owners, places = donor_plan(key)
    return owners


def draw_donor_offset(key, part):
    owners, places = donor_plan(key)
    return places


def draw_fields(key, part):
    key = jax.random.fold_in(key, 11)
    key_scale, key_values = jax.random.split(key)
    column_scale = jnp.exp(jax.random.uniform(key_scale, (1, NX, NY, 1), jnp.float32, math.log(0.3), math.log(3.0)))
    base = jnp.clip(jax.random.normal(key_values, (FIELDS, NX, NY, NZ), jnp.float32), -4.0, 4.0)
    return (base * column_scale).astype(jnp.float32)


def plant(result, rng, least, largest):
    longest = result.shape.index(max(result.shape))
    spots = []
    for shift in (0, 1):
        where = [jax.random.randint(jax.random.fold_in(rng, axis), (), 0, length) for axis, length in enumerate(result.shape)]
        where[longest] = (where[longest] + shift) % result.shape[longest]
        spots.append(tuple(where))
    return result.at[spots[0]].set(least).at[spots[1]].set(largest)


def level_of(rng, dims, shards, low, top_value):
    def one(position, shards_of):
        steps = jax.random.uniform(jax.random.fold_in(jax.random.fold_in(rng, 6), position), (shards_of,), jnp.float32, low / len(shards), top_value / len(shards))
        return jnp.repeat(jnp.exp(steps), dims[position] // shards_of).reshape((-1,) + (1,) * (len(dims) - position - 1))

    gain = one(*shards[0])
    for cut in shards[1:]:
        gain = gain * one(*cut)
    return gain


def setup_inputs(seed: int = 0) -> dict:
    arg_keys = jax.random.split(jax.random.key(seed), 6)
    return {
        "fields": draw_fields(jax.random.fold_in(arg_keys[5], 71), 0),
        "displacement": jnp.clip(jax.random.uniform(arg_keys[1], (2, NX, NY), jnp.float32, -0.3, 0.3) * level_of(arg_keys[1], (2, NX, NY), ((1, 32), (2, 16)), -0.4, 0.0), -0.3, 0.3),
        "donor_tile": draw_donor_tile(jax.random.fold_in(arg_keys[5], 71), 0),
        "donor_offset": draw_donor_offset(jax.random.fold_in(arg_keys[5], 71), 0),
        "donor_count": plant(jax.random.randint(arg_keys[4], (NX, NY), 1, DONORS + 1), jax.random.fold_in(arg_keys[4], 1), 1, DONORS).astype(jnp.int32),
    }


BETA_COEF = 0.5
OMEGA_COEF = 0.6
SPREAD_SQ = 64.0

def monitor_core(density_pad):
    east_diff = density_pad[2:, 1:-1] - density_pad[:-2, 1:-1]
    north_diff = density_pad[1:-1, 2:] - density_pad[1:-1, :-2]
    steepness = lax.optimization_barrier(jnp.mean(east_diff * east_diff + north_diff * north_diff, axis=-1))
    return jnp.sqrt(1.0 + BETA_COEF * steepness)

def sweep_core(moved_pad, monitor_pad, interior):
    centre_monitor = monitor_pad[1:-1, 1:-1]
    east_weight = 0.5 * (centre_monitor + monitor_pad[2:, 1:-1])
    west_weight = 0.5 * (centre_monitor + monitor_pad[:-2, 1:-1])
    north_weight = 0.5 * (centre_monitor + monitor_pad[1:-1, 2:])
    south_weight = 0.5 * (centre_monitor + monitor_pad[1:-1, :-2])
    total_weight = east_weight + west_weight + north_weight + south_weight
    blended = (east_weight * moved_pad[:, 2:, 1:-1] + west_weight * moved_pad[:, :-2, 1:-1] + north_weight * moved_pad[:, 1:-1, 2:] + south_weight * moved_pad[:, 1:-1, :-2]) / total_weight
    drift = jnp.stack([(east_weight - west_weight) / total_weight, (north_weight - south_weight) / total_weight])
    centre = moved_pad[:, 1:-1, 1:-1]
    relaxed = (1.0 - OMEGA_COEF) * centre + OMEGA_COEF * (blended + drift)
    return jnp.where(interior, relaxed, centre)

def remap_global(fields, old_disp, new_disp, donor_tile, donor_offset, donor_count):
    column_table = fields.reshape(FIELDS, NX * NY, NZ)
    old_flat = old_disp.reshape(2, NX * NY)
    row_index = jnp.arange(NX, dtype=jnp.int32)[:, None]
    col_index = jnp.arange(NY, dtype=jnp.int32)[None, :]
    weighted_sum = jnp.zeros((FIELDS, NX, NY, NZ), jnp.float32)
    weight_sum = jnp.zeros((NX, NY), jnp.float32)
    for donor_slot in range(DONORS):
        owner_tile = donor_tile[:, :, donor_slot]
        place = donor_offset[:, :, donor_slot]
        source_row = owner_tile * CX + place // CY
        source_col = col_index // CY * CY + place % CY
        flat_index = (source_row * NY + source_col).reshape(-1).astype(jnp.int32)
        donor_values = jnp.take(column_table, flat_index, axis=1).reshape(FIELDS, NX, NY, NZ)
        donor_disp = jnp.take(old_flat, flat_index, axis=1).reshape(2, NX, NY)
        delta_x = (row_index - source_row).astype(jnp.float32) + (new_disp[0] - donor_disp[0])
        delta_y = (col_index - source_col).astype(jnp.float32) + (new_disp[1] - donor_disp[1])
        weight = jnp.where(donor_slot < donor_count, 1.0 / (1.0 + (delta_x * delta_x + delta_y * delta_y) / SPREAD_SQ), 0.0)
        weighted_sum = weighted_sum + weight[None, :, :, None] * donor_values
        weight_sum = weight_sum + weight
    return weighted_sum / weight_sum[None, :, :, None]

def reference(fields, displacement, donor_tile, donor_offset, donor_count):
    row_index = jnp.arange(NX, dtype=jnp.int32)
    col_index = jnp.arange(NY, dtype=jnp.int32)
    interior = ((row_index >= 1) & (row_index <= NX - 2))[:, None] & ((col_index >= 1) & (col_index <= NY - 2))[None, :]
    for step_index in range(STEPS):
        density_pad = jnp.pad(fields[0], ((1, 1), (1, 1), (0, 0)))
        monitor_pad = jnp.pad(monitor_core(density_pad), 1)
        moved = displacement
        for sweep_index in range(SWEEPS):
            moved = sweep_core(jnp.pad(moved, ((0, 0), (1, 1), (1, 1))), monitor_pad, interior)
        fields = remap_global(fields, displacement, moved, donor_tile, donor_offset, donor_count)
        displacement = moved
    return (displacement, fields)
```

```python
import jax
import jax.numpy as jnp
from jax import lax
from jax.experimental import pallas as pl
from jax.experimental.pallas import tpu as pltpu
from jax.sharding import PartitionSpec as P

CX = 16
CY = 32
NZ = 128
FIELDS = 8
DONORS = 4
CAP = 32
SWEEPS = 3
STEPS = 2
NX = 512
NY = 512

BETA_COEF = 0.5
OMEGA_COEF = 0.6
SPREAD_SQ = 64.0

TILE = CX * CY
HALO = 4
EXT = CX + 2 * HALO
SIDE = 8
WIDE = CY + 2 * SIDE
HALF = 64
LANES = 128
EDGE = HALO * CY
AT_OFFSETS = EDGE
AT_REST = EDGE + 8
DONOR_ROWS = FIELDS * CAP
REQUEST_MSG = AT_REST + 8
DONOR_MSG = DONOR_ROWS + 8
FULL_MSG = AT_REST + DONOR_MSG
Y_DENSITY = EXT * HALO
Y_MSG = Y_DENSITY + EXT

F32 = jnp.float32
BF16 = jnp.bfloat16
VMEM_BYTES = 56 * 1024 * 1024


def iota(shape, dim):
    return lax.broadcasted_iota(jnp.int32, shape, dim)


def pick(flag, a, b):
    return jnp.where(jnp.full(a.shape, flag, jnp.int32) != 0, a, b)


def widen(x):
    return jnp.concatenate([x, jnp.zeros((x.shape[0], LANES - x.shape[1]), x.dtype)], axis=1)


def spread(x, y):
    gap = jnp.zeros((CX, CY), F32)
    return pltpu.roll(jnp.concatenate([x, gap, y, gap], axis=1), SIDE, 1)


def parities():
    tile_x = lax.axis_index("gx")
    tile_y = lax.axis_index("gy")
    return tile_x, tile_y, lax.rem(tile_x, 2), lax.rem(tile_y, 2)


def first_kernel(disp, head, tail, owner, place, out_even, out_odd, own, aux):
    tile_x, _, px, _ = parities()
    offsets = spread(disp[0], disp[1])
    own[...] = offsets
    first_owner = owner[:, 0, :]
    to_left = widen((first_owner == tile_x - 1).astype(F32))
    to_right = widen((first_owner == tile_x + 1).astype(F32))
    marks = jnp.concatenate([to_left, to_right], axis=0)
    earlier = (iota((LANES, LANES), 0) < iota((LANES, LANES), 1)).astype(F32)
    in_row = jnp.dot(marks, earlier, preferred_element_type=F32)
    totals = jnp.broadcast_to(jnp.sum(marks, axis=1, keepdims=True), (2 * CX, LANES))
    row = lax.rem(iota((2 * CX, LANES), 0), CX)
    before = totals
    for step in (1, 2, 4, 8):
        before = before + jnp.where(row >= step, pltpu.roll(before, step, 0), 0.0)
    rank = in_row + before - totals
    code = jnp.where(
        to_left > 0, rank[:CX], jnp.where(to_right > 0, rank[CX:] + CAP, -1.0)
    )
    aux[:CX, :] = code
    columns = jnp.transpose(jnp.concatenate([code, widen(place[:, 0, :].astype(F32))], axis=0))
    lane = iota((CY, LANES), 1).astype(F32)
    asked = jnp.zeros((CY, LANES), F32)
    for r in range(CX):
        asked = asked + jnp.where(
            columns[:CY, r : r + 1] == lane, columns[:CY, CX + r : CX + r + 1], 0.0
        )
    request = jnp.broadcast_to(jnp.sum(asked, axis=0, keepdims=True), (8, LANES))
    aux[CX:, :] = request
    low, high = head[0], tail[0]
    out_even[:EDGE, :] = pick(px, low, high)
    out_odd[:EDGE, :] = pick(px, high, low)
    low, high = offsets[:8], offsets[8:]
    out_even[AT_OFFSETS:AT_REST, :] = pick(px, low, high)
    out_odd[AT_OFFSETS:AT_REST, :] = pick(px, high, low)
    out_even[AT_REST:, :] = request
    out_odd[AT_REST:, :] = request


def fill_offsets(ext, own, left, right):
    ext[0:HALO, :] = left[HALO:8]
    ext[HALO : HALO + CX, :] = own
    ext[HALO + CX :, :] = right[0:HALO]


def edge_columns(density, from_left, from_right, start):
    parts = []
    for part, rows in ((from_left, HALO), (density, CX), (from_right, HALO)):
        parts.append(part.reshape(rows, CY, NZ)[:, start : start + 8, :])
    return jnp.concatenate(parts, axis=0)


def pack_y(density, halo_even, halo_odd, own, ext, px, py, out_even, out_odd):
    from_left = pick(px, halo_even[:EDGE, :], halo_odd[:EDGE, :])
    from_right = pick(px, halo_odd[:EDGE, :], halo_even[:EDGE, :])
    even = halo_even[AT_OFFSETS:AT_REST, :]
    odd = halo_odd[AT_OFFSETS:AT_REST, :]
    fill_offsets(ext, own, pick(px, even, odd), pick(px, odd, even))
    half = EXT // 2
    low = edge_columns(density, from_left, from_right, 0)
    high = edge_columns(density, from_left, from_right, CY - 8)
    sub = iota((half, 8, NZ), 1)
    low = jnp.where(sub < HALO, low[:half], pltpu.roll(low[half:], HALO, 1))
    high = jnp.where(sub < HALO, pltpu.roll(high[:half], HALO, 1), high[half:])
    low = low.reshape(Y_DENSITY, NZ)
    high = high.reshape(Y_DENSITY, NZ)
    out_even[:Y_DENSITY, :] = pick(py, low, high)
    out_odd[:Y_DENSITY, :] = pick(py, high, low)
    out_even[Y_DENSITY:, :] = ext[...]
    out_odd[Y_DENSITY:, :] = ext[...]


def take_donors(fields, places, out_even, out_odd, start):
    def one(r, carry):
        for out, shift in ((out_even, 0), (out_odd, CAP)):
            p = places[0, r + shift]
            for f in range(FIELDS):
                out[pl.ds(start + f * CAP + r, 1), :] = fields[f, pl.ds(p, 1), :]
        return carry

    lax.fori_loop(0, CAP, one, 0, unroll=8)


def flat_rows(wide):
    row = iota((CX, LANES), 0)
    lane = iota((CX, LANES), 1)
    outs = []
    for base in (SIDE, HALF + SIDE):
        pieces = jnp.zeros((CX, LANES), F32)
        for m in range(4):
            moved = pltpu.roll(wide, (m * CY - base) % LANES, 1)
            pieces = pieces + jnp.where((row % 4 == m) & (lane // CY == m), moved, 0.0)
        quarters = [
            jnp.sum(jnp.where(row // 4 == q, pieces, 0.0), axis=0, keepdims=True) for q in range(4)
        ]
        outs.append(jnp.concatenate(quarters, axis=1))
    return outs


def donor_offsets(own, asked, out_even, out_odd, start):
    flat_x, flat_y = flat_rows(own)
    sub = iota((HALF, LANES), 0)
    lane = iota((HALF, LANES), 1)
    wanted = jnp.sum(
        jnp.where(sub == lane, jnp.broadcast_to(asked, (HALF, LANES)), 0.0), axis=1, keepdims=True
    )
    hit = wanted == iota((HALF, TILE), 1).astype(F32)
    rows = []
    for flat in (flat_x, flat_y):
        column = jnp.sum(jnp.where(hit, flat, 0.0), axis=1, keepdims=True)
        rows.append(jnp.sum(jnp.where(sub == lane, column, 0.0), axis=0, keepdims=True))
    place = iota((8, LANES), 0)
    even = jnp.where(place == 0, rows[0], jnp.where(place == 1, rows[1], 0.0))
    out_even[start : start + 8, :] = even
    out_odd[start : start + 8, :] = pltpu.roll(even, LANES - CAP, 1)


def second_kernel(
    fields, own, halo_even, halo_odd, y_even, y_odd, donor_even, donor_odd, asked_out, ext, places, sem
):
    _, _, px, py = parities()
    lane = iota((8, LANES), 1)
    even = halo_even[AT_REST:, :]
    odd = halo_odd[AT_REST:, :]
    asked = pick(
        px,
        jnp.where(lane < CAP, pltpu.roll(even, LANES - CAP, 1), pltpu.roll(odd, CAP, 1)),
        jnp.where(lane < CAP, even, odd),
    )
    asked_out[...] = asked.astype(jnp.int32)
    copy = pltpu.make_async_copy(asked_out, places, sem)
    copy.start()
    pack_y(fields[0], halo_even, halo_odd, own[...], ext, px, py, y_even, y_odd)
    donor_offsets(own[...], asked[:1], donor_even, donor_odd, DONOR_ROWS)
    copy.wait()
    take_donors(fields, places, donor_even, donor_odd, 0)


def third_kernel(density, own, halo_even, halo_odd, y_even, y_odd, ext):
    _, _, px, py = parities()
    pack_y(density[0], halo_even, halo_odd, own[...], ext, px, py, y_even, y_odd)


def relax(fields, own, halo_even, halo_odd, y_even, y_odd, dens, ext, mon):
    tile_x, tile_y, px, py = parities()
    dens[HALO : HALO + CX, SIDE : SIDE + CY, :] = fields[0].reshape(CX, CY, NZ)
    left = pick(px, halo_even[:EDGE, :], halo_odd[:EDGE, :])
    right = pick(px, halo_odd[:EDGE, :], halo_even[:EDGE, :])
    dens[:HALO, SIDE : SIDE + CY, :] = left.reshape(HALO, CY, NZ)
    dens[HALO + CX :, SIDE : SIDE + CY, :] = right.reshape(HALO, CY, NZ)
    half = EXT // 2
    below = pick(py, y_even[:Y_DENSITY, :], y_odd[:Y_DENSITY, :]).reshape(half, 8, NZ)
    above = pick(py, y_odd[:Y_DENSITY, :], y_even[:Y_DENSITY, :]).reshape(half, 8, NZ)
    dens[:half, :SIDE, :] = pltpu.roll(below, HALO, 1)
    dens[half:, :SIDE, :] = below
    dens[:half, SIDE + CY :, :] = above
    dens[half:, SIDE + CY :, :] = pltpu.roll(above, HALO, 1)

    even = halo_even[AT_OFFSETS:AT_REST, :]
    odd = halo_odd[AT_OFFSETS:AT_REST, :]
    fill_offsets(ext, own, pick(px, even, odd), pick(px, odd, even))
    lane = iota((EXT, LANES), 1)
    half_lane = lax.rem(lane, HALF)
    even = y_even[Y_DENSITY:, :]
    odd = y_odd[Y_DENSITY:, :]
    moved = ext[...]
    moved = jnp.where(half_lane < SIDE, pltpu.roll(pick(py, even, odd), LANES - CY, 1), moved)
    moved = jnp.where(half_lane >= SIDE + CY, pltpu.roll(pick(py, odd, even), CY, 1), moved)

    spot = iota((WIDE, LANES), 0)
    diagonal = spot == lax.rem(iota((WIDE, LANES), 1), HALF)
    mon[0:1, :] = jnp.zeros((1, LANES), F32)
    mon[EXT - 1 :, :] = jnp.zeros((1, LANES), F32)
    for r in range(1, EXT - 1):
        east = dens[r + 1] - dens[r - 1]
        here = dens[r]
        north = pltpu.roll(here, WIDE - 1, 0) - pltpu.roll(here, 1, 0)
        steep = jnp.sum(east * east + north * north, axis=1, keepdims=True)
        mon[r : r + 1, :] = jnp.sum(jnp.where(diagonal, steep, 0.0), axis=0, keepdims=True)
    row_global = tile_x * CX - HALO + iota((EXT, LANES), 0)
    col_global = tile_y * CY - SIDE + half_lane
    on_grid = (row_global >= 0) & (row_global < NX) & (col_global >= 0) & (col_global < NY)
    interior = (
        (row_global >= 1) & (row_global <= NX - 2) & (col_global >= 1) & (col_global <= NY - 2)
    )
    monitor = jnp.where(on_grid, jnp.sqrt(1.0 + (BETA_COEF / NZ) * mon[...]), 0.0)

    def to_east(x):
        return pltpu.roll(x, EXT - 1, 0)

    def to_west(x):
        return pltpu.roll(x, 1, 0)

    def to_north(x):
        return pltpu.roll(x, LANES - 1, 1)

    def to_south(x):
        return pltpu.roll(x, 1, 1)

    east = monitor + to_east(monitor)
    west = monitor + to_west(monitor)
    north = monitor + to_north(monitor)
    south = monitor + to_south(monitor)
    scale = OMEGA_COEF / (east + west + north + south)
    drift = jnp.where(lane < HALF, east - west, north - south) * scale
    east = east * scale
    west = west * scale
    north = north * scale
    south = south * scale
    for _ in range(SWEEPS):
        relaxed = (
            (1.0 - OMEGA_COEF) * moved
            + east * to_east(moved)
            + west * to_west(moved)
            + north * to_north(moved)
            + south * to_south(moved)
            + drift
        )
        moved = jnp.where(interior, relaxed, moved)
    ext[...] = moved
    return ext[HALO : HALO + CX, :]


def weigh(own, moved, owner, place, count, aux, offsets_even, offsets_odd, left_hand, inverse):
    tile_x, _, px, _ = parities()
    flat_x, flat_y = flat_rows(own)
    spot = iota((1, TILE), 1)
    flat_x = flat_x + (spot // CY).astype(F32)
    flat_y = flat_y + lax.rem(spot, CY).astype(F32)

    request = aux[CX : CX + 1, :].astype(jnp.int32)
    lane = iota((1, LANES), 1)
    even, odd = offsets_even, offsets_odd
    left = pick(px, even, odd)
    right = pick(px, odd, even)
    far = jnp.where(iota((8, LANES), 1) < CAP, left, pltpu.roll(right, CAP, 1))
    far_x = far[0:1] + jnp.where(lane < CAP, request // CY - CX, request // CY + CX).astype(F32)
    far_y = far[1:2] + lax.rem(request, CY).astype(F32)
    far_x = jnp.where(lane < HALF, far_x, pltpu.roll(far_x, HALF, 1))
    far_y = jnp.where(lane < HALF, far_y, pltpu.roll(far_y, HALF, 1))
    far_lane = lax.rem(lane, HALF).astype(F32)
    near_half = iota((CY, LANES), 1) < HALF

    live = count[...]
    codes = []
    for k in range(DONORS):
        here = owner[:, k, :] == tile_x
        codes.append(widen(jnp.where(here & (k < live), place[:, k, :], -1).astype(F32)))
    codes.append(jnp.where(widen(live.astype(F32)) > 0, aux[:CX, :], -1.0))
    columns = jnp.transpose(jnp.concatenate(codes, axis=0))
    shifts = jnp.transpose(moved)
    along = iota((CY, 1), 0).astype(F32)
    spots = iota((CY, TILE), 1).astype(F32)

    def weight(dx, dy):
        bulk = SPREAD_SQ + dx * dx + dy * dy
        guess = pl.reciprocal(bulk, approx=True)
        return guess * (2.0 - bulk * guess)

    for r in range(CX):
        at_x = shifts[SIDE : SIDE + CY, r : r + 1] + float(r)
        at_y = shifts[HALF + SIDE : HALF + SIDE + CY, r : r + 1] + along
        dense = weight(at_x - flat_x, at_y - flat_y)
        total = jnp.zeros((CY, TILE), F32)
        for k in range(DONORS):
            code = columns[:CY, k * CX + r : k * CX + r + 1]
            total = total + jnp.where(code == spots, dense, 0.0)
        code = columns[:CY, DONORS * CX + r : DONORS * CX + r + 1]
        remote = jnp.where(code == far_lane, weight(at_x - far_x, at_y - far_y), 0.0)
        norm = jnp.sum(total, axis=1, keepdims=True) + jnp.sum(
            jnp.where(near_half, remote, 0.0), axis=1, keepdims=True
        )
        rows = slice(r * CY, (r + 1) * CY)
        inverse[rows, :] = jnp.broadcast_to(1.0 / norm, (CY, LANES))
        high = total.astype(BF16)
        left_hand[rows, 0:TILE] = high
        left_hand[rows, TILE : 2 * TILE] = (total - high.astype(F32)).astype(BF16)
        left_hand[rows, 2 * TILE : 3 * TILE] = high
        high = remote.astype(BF16)
        low = (remote - high.astype(F32)).astype(BF16)
        base = 3 * TILE
        left_hand[rows, base : base + LANES] = jnp.where(near_half, high.astype(F32), low.astype(F32)).astype(BF16)
        left_hand[rows, base + LANES : base + 2 * LANES] = jnp.where(near_half, high.astype(F32), 0.0).astype(BF16)


def split(x):
    high = x.astype(BF16)
    return high, (x - high.astype(F32)).astype(BF16)


def combine(fields, donors_even, donors_odd, px, left_hand, right_hand, inverse, out):
    for f in range(FIELDS):
        n, lanes = f // 2, slice((f % 2) * NZ, (f % 2) * NZ + NZ)
        high, low = split(fields[f])
        right_hand[n, 0:TILE, lanes] = high
        right_hand[n, TILE : 2 * TILE, lanes] = high
        right_hand[n, 2 * TILE : 3 * TILE, lanes] = low
        even = donors_even(f)
        odd = donors_odd(f)
        both = jnp.concatenate([pick(px, even, odd), pick(px, odd, even)], axis=0)
        high, low = split(both)
        base = 3 * TILE
        right_hand[n, base : base + HALF, lanes] = high
        right_hand[n, base + HALF : base + 2 * HALF, lanes] = high
        right_hand[n, base + 2 * HALF : base + 3 * HALF, lanes] = low
        right_hand[n, base + 3 * HALF : base + 4 * HALF, lanes] = jnp.zeros((HALF, NZ), BF16)

    for n in range(FIELDS // 2):
        mixed = jnp.dot(left_hand[...], right_hand[n], preferred_element_type=F32)
        out[2 * n] = mixed[:, :NZ] * inverse[...]
        out[2 * n + 1] = mixed[:, NZ:] * inverse[...]


def step_kernel(
    fields, own, halo_even, halo_odd, y_even, y_odd, donor_even, donor_odd, owner, place, count, aux, asked,
    out, own_out, x_even, x_odd,
    dens, ext, mon, left_hand, right_hand, inverse, places, sem,
):
    _, _, px, _ = parities()
    copy = pltpu.make_async_copy(asked, places, sem)
    copy.start()
    moved = relax(fields, own[...], halo_even, halo_odd, y_even, y_odd, dens, ext, mon)
    own_out[...] = moved
    weigh(
        own[...], moved, owner, place, count, aux,
        donor_even[DONOR_ROWS:, :], donor_odd[DONOR_ROWS:, :], left_hand, inverse,
    )
    combine(
        fields,
        lambda f: donor_even[f * CAP : (f + 1) * CAP, :],
        lambda f: donor_odd[f * CAP : (f + 1) * CAP, :],
        px, left_hand, right_hand, inverse, out,
    )
    low, high = out[0, :EDGE, :], out[0, TILE - EDGE :, :]
    x_even[:EDGE, :] = pick(px, low, high)
    x_odd[:EDGE, :] = pick(px, high, low)
    low, high = moved[:8], moved[8:]
    x_even[AT_OFFSETS:AT_REST, :] = pick(px, low, high)
    x_odd[AT_OFFSETS:AT_REST, :] = pick(px, high, low)
    donor_offsets(moved, asked[:1, :].astype(F32), x_even, x_odd, AT_REST + DONOR_ROWS)
    copy.wait()
    take_donors(out, places, x_even, x_odd, AT_REST)


def last_kernel(
    fields, own, x_even, x_odd, y_even, y_odd, owner, place, count, aux,
    moved_out, out,
    dens, ext, mon, left_hand, right_hand, inverse,
):
    _, _, px, _ = parities()
    moved = relax(fields, own[...], x_even, x_odd, y_even, y_odd, dens, ext, mon)
    moved_out[0] = pltpu.roll(moved, LANES - SIDE, 1)[:, :CY]
    moved_out[1] = pltpu.roll(moved, HALF - SIDE, 1)[:, :CY]
    at = AT_REST + DONOR_ROWS
    weigh(
        own[...], moved, owner, place, count, aux,
        x_even[at : at + 8, :], x_odd[at : at + 8, :], left_hand, inverse,
    )
    combine(
        fields,
        lambda f: x_even[AT_REST + f * CAP : AT_REST + (f + 1) * CAP, :],
        lambda f: x_odd[AT_REST + f * CAP : AT_REST + (f + 1) * CAP, :],
        px, left_hand, right_hand, inverse, out,
    )


def shape(*dims, dtype=F32):
    return jax.ShapeDtypeStruct(dims, dtype)


def call(kernel, outs, scratch=(), in_specs=None, name=None):
    extra = {} if in_specs is None else {"in_specs": in_specs, "grid": (1,)}
    return pl.pallas_call(
        kernel,
        out_shape=outs,
        scratch_shapes=list(scratch),
        compiler_params=pltpu.CompilerParams(vmem_limit_bytes=VMEM_BYTES),
        name=name,
        **extra,
    )


def swap_pairs(block, axis, odd):
    count = lax.axis_size(axis)
    route = []
    for a in range(1 if odd else 0, count - 1, 2):
        route += [(a, a + 1), (a + 1, a)]
    return lax.ppermute(block, axis, route)


def swap(even, odd, axis):
    return swap_pairs(even, axis, False), swap_pairs(odd, axis, True)


WORK = (
    pltpu.VMEM((EXT, WIDE, NZ), F32),
    pltpu.VMEM((EXT, LANES), F32),
    pltpu.VMEM((EXT, LANES), F32),
    pltpu.VMEM((TILE, 3 * TILE + 4 * HALF), BF16),
    pltpu.VMEM((FIELDS // 2, 3 * TILE + 4 * HALF, 2 * NZ), BF16),
    pltpu.VMEM((TILE, LANES), F32),
)
PLACES = (pltpu.SMEM((8, LANES), jnp.int32), pltpu.SemaphoreType.DMA)


def whole():
    return pl.BlockSpec(memory_space=pltpu.VMEM)


def density_rows(start, rows):
    return pl.BlockSpec((1, rows, NZ), lambda i: (0, start // rows, 0))


def per_device(fields, displacement, donor_tile, donor_offset, donor_count):
    fields = fields.reshape(FIELDS, TILE, NZ)
    owner = donor_tile.transpose(0, 2, 1)
    place = donor_offset.transpose(0, 2, 1)
    even, odd, own, aux = call(
        first_kernel,
        (shape(REQUEST_MSG, LANES), shape(REQUEST_MSG, LANES), shape(CX, LANES), shape(CX + 8, LANES)),
        in_specs=[whole(), density_rows(0, EDGE), density_rows(TILE - EDGE, EDGE), whole(), whole()],
        name="pack_first",
    )(displacement, fields, fields, owner, place)
    halo = swap(even, odd, "gx")
    y_even, y_odd, d_even, d_odd, asked = call(
        second_kernel,
        (
            shape(Y_MSG, LANES), shape(Y_MSG, LANES), shape(DONOR_MSG, LANES), shape(DONOR_MSG, LANES),
            shape(8, LANES, dtype=jnp.int32),
        ),
        scratch=(pltpu.VMEM((EXT, LANES), F32),) + PLACES,
        name="pack_donors",
    )(fields, own, *halo)
    y_halo = swap(y_even, y_odd, "gy")
    donors = swap(d_even, d_odd, "gx")
    fields, own, even, odd = call(
        step_kernel,
        (shape(FIELDS, TILE, NZ), shape(CX, LANES), shape(FULL_MSG, LANES), shape(FULL_MSG, LANES)),
        scratch=WORK + PLACES,
        name="step_one",
    )(fields, own, *halo, *y_halo, *donors, owner, place, donor_count, aux, asked)
    halo = swap(even, odd, "gx")
    y_even, y_odd = call(
        third_kernel,
        (shape(Y_MSG, LANES), shape(Y_MSG, LANES)),
        scratch=(pltpu.VMEM((EXT, LANES), F32),),
        in_specs=[density_rows(0, TILE), whole(), whole(), whole()],
        name="pack_y",
    )(fields, own, *halo)
    y_halo = swap(y_even, y_odd, "gy")
    moved, fields = call(
        last_kernel,
        (shape(2, CX, CY), shape(FIELDS, TILE, NZ)),
        scratch=WORK,
        name="step_two",
    )(fields, own, *halo, *y_halo, owner, place, donor_count, aux)
    return moved, fields.reshape(FIELDS, CX, CY, NZ)


def solution(mesh):
    return jax.shard_map(
        per_device,
        mesh=mesh,
        in_specs=(
            P(None, "gx", "gy", None),
            P(None, "gx", "gy"),
            P("gx", "gy", None),
            P("gx", "gy", None),
            P("gx", "gy"),
        ),
        out_specs=(P(None, "gx", "gy"), P(None, "gx", "gy", None)),
        check_vma=False,
    )
```

```python
import jax
import jax.numpy as jnp
from jax import lax
from jax.experimental import pallas as pl
from jax.experimental.pallas import tpu as pltpu
from jax.sharding import PartitionSpec as P

CX = 16
CY = 32
NZ = 128
FIELDS = 8
DONORS = 4
CAP = 32
SWEEPS = 3
STEPS = 2
NX = 512
NY = 512

BETA_COEF = 0.5
OMEGA_COEF = 0.6
SPREAD_SQ = 64.0

TILE = CX * CY
HALO = 4
EXT = CX + 2 * HALO
SIDE = 8
WIDE = CY + 2 * SIDE
HALF = 64
LANES = 128
EDGE = HALO * CY
AT_OFFSETS = EDGE
AT_REST = EDGE + 8
DONOR_ROWS = FIELDS * CAP
REQUEST_MSG = AT_REST + 8
DONOR_MSG = DONOR_ROWS + 8
Y_DENSITY = EXT * HALO
Y_MSG = Y_DENSITY + EXT

F32 = jnp.float32
BF16 = jnp.bfloat16
VMEM_BYTES = 20 * 1024 * 1024


def iota(shape, dim):
    return lax.broadcasted_iota(jnp.int32, shape, dim)


def pick(flag, a, b):
    return jnp.where(jnp.full(a.shape, flag, jnp.int32) != 0, a, b)


def widen(x):
    return jnp.concatenate([x, jnp.zeros((x.shape[0], LANES - x.shape[1]), x.dtype)], axis=1)


def spread(x, y):
    gap = jnp.zeros((CX, CY), F32)
    return pltpu.roll(jnp.concatenate([x, gap, y, gap], axis=1), SIDE, 1)


def parities():
    tile_x = lax.axis_index("gx")
    tile_y = lax.axis_index("gy")
    return tile_x, tile_y, lax.rem(tile_x, 2), lax.rem(tile_y, 2)


def first_kernel(
    disp_hbm, fields_hbm, owner_hbm, place_hbm, out_even, out_odd, own, aux, disp, head, tail, owner, place, sems
):
    tile_x, _, px, _ = parities()
    copies = [
        pltpu.make_async_copy(source, target, sems.at[i])
        for i, (source, target) in enumerate(
            (
                (owner_hbm, owner),
                (place_hbm, place),
                (disp_hbm, disp),
                (fields_hbm.at[0, pl.ds(0, EDGE)], head),
                (fields_hbm.at[0, pl.ds(TILE - EDGE, EDGE)], tail),
            )
        )
    ]
    for copy in copies:
        copy.start()
    for copy in copies:
        copy.wait()
    offsets = spread(disp[0], disp[1])
    own[...] = offsets
    first_owner = owner[:, 0, :]
    to_left = widen((first_owner == tile_x - 1).astype(F32))
    to_right = widen((first_owner == tile_x + 1).astype(F32))
    marks = jnp.concatenate([to_left, to_right], axis=0)
    earlier = (iota((LANES, LANES), 0) < iota((LANES, LANES), 1)).astype(F32)
    in_row = jnp.dot(marks, earlier, preferred_element_type=F32)
    totals = jnp.broadcast_to(jnp.sum(marks, axis=1, keepdims=True), (2 * CX, LANES))
    row = lax.rem(iota((2 * CX, LANES), 0), CX)
    before = totals
    for step in (1, 2, 4, 8):
        before = before + jnp.where(row >= step, pltpu.roll(before, step, 0), 0.0)
    rank = in_row + before - totals
    code = jnp.where(
        to_left > 0, rank[:CX], jnp.where(to_right > 0, rank[CX:] + CAP, -1.0)
    )
    aux[:CX, :] = code
    columns = jnp.transpose(jnp.concatenate([code, widen(place[:, 0, :].astype(F32))], axis=0))
    lane = iota((CY, LANES), 1).astype(F32)
    asked = jnp.zeros((CY, LANES), F32)
    for r in range(CX):
        asked = asked + jnp.where(
            columns[:CY, r : r + 1] == lane, columns[:CY, CX + r : CX + r + 1], 0.0
        )
    request = jnp.broadcast_to(jnp.sum(asked, axis=0, keepdims=True), (8, LANES))
    aux[CX:, :] = request
    low, high = head[...], tail[...]
    out_even[:EDGE, :] = pick(px, low, high)
    out_odd[:EDGE, :] = pick(px, high, low)
    low, high = offsets[:8], offsets[8:]
    out_even[AT_OFFSETS:AT_REST, :] = pick(px, low, high)
    out_odd[AT_OFFSETS:AT_REST, :] = pick(px, high, low)
    out_even[AT_REST:, :] = request
    out_odd[AT_REST:, :] = request


def fill_offsets(ext, own, left, right):
    ext[0:HALO, :] = left[HALO:8]
    ext[HALO : HALO + CX, :] = own
    ext[HALO + CX :, :] = right[0:HALO]


def edge_columns(density, from_left, from_right, start):
    parts = []
    for part, rows in ((from_left, HALO), (density, CX), (from_right, HALO)):
        parts.append(part.reshape(rows, CY, NZ)[:, start : start + 8, :])
    return jnp.concatenate(parts, axis=0)


def pack_y(density, halo_even, halo_odd, own, ext, px, py, out_even, out_odd):
    from_left = pick(px, halo_even[:EDGE, :], halo_odd[:EDGE, :])
    from_right = pick(px, halo_odd[:EDGE, :], halo_even[:EDGE, :])
    even = halo_even[AT_OFFSETS:AT_REST, :]
    odd = halo_odd[AT_OFFSETS:AT_REST, :]
    fill_offsets(ext, own, pick(px, even, odd), pick(px, odd, even))
    half = EXT // 2
    low = edge_columns(density, from_left, from_right, 0)
    high = edge_columns(density, from_left, from_right, CY - 8)
    sub = iota((half, 8, NZ), 1)
    low = jnp.where(sub < HALO, low[:half], pltpu.roll(low[half:], HALO, 1))
    high = jnp.where(sub < HALO, pltpu.roll(high[:half], HALO, 1), high[half:])
    low = low.reshape(Y_DENSITY, NZ)
    high = high.reshape(Y_DENSITY, NZ)
    out_even[:Y_DENSITY, :] = pick(py, low, high)
    out_odd[:Y_DENSITY, :] = pick(py, high, low)
    out_even[Y_DENSITY:, :] = ext[...]
    out_odd[Y_DENSITY:, :] = ext[...]


def take_donors(fields, places, out_even, out_odd):
    def one(r, carry):
        for out, shift in ((out_even, 0), (out_odd, CAP)):
            p = places[0, r + shift]
            for f in range(FIELDS):
                out[pl.ds(f * CAP + r, 1), :] = fields[f, pl.ds(p, 1), :]
        return carry

    lax.fori_loop(0, CAP, one, 0, unroll=8)


def flat_rows(wide):
    row = iota((CX, LANES), 0)
    lane = iota((CX, LANES), 1)
    outs = []
    for base in (SIDE, HALF + SIDE):
        pieces = jnp.zeros((CX, LANES), F32)
        for m in range(4):
            moved = pltpu.roll(wide, (m * CY - base) % LANES, 1)
            pieces = pieces + jnp.where((row % 4 == m) & (lane // CY == m), moved, 0.0)
        quarters = [
            jnp.sum(jnp.where(row // 4 == q, pieces, 0.0), axis=0, keepdims=True) for q in range(4)
        ]
        outs.append(jnp.concatenate(quarters, axis=1))
    return outs


def donor_offsets(own, asked, out_even, out_odd):
    flat_x, flat_y = flat_rows(own)
    sub = iota((HALF, LANES), 0)
    lane = iota((HALF, LANES), 1)
    wanted = jnp.sum(
        jnp.where(sub == lane, jnp.broadcast_to(asked, (HALF, LANES)), 0.0), axis=1, keepdims=True
    )
    hit = wanted == iota((HALF, TILE), 1).astype(F32)
    rows = []
    for flat in (flat_x, flat_y):
        column = jnp.sum(jnp.where(hit, flat, 0.0), axis=1, keepdims=True)
        rows.append(jnp.sum(jnp.where(sub == lane, column, 0.0), axis=0, keepdims=True))
    place = iota((8, LANES), 0)
    even = jnp.where(place == 0, rows[0], jnp.where(place == 1, rows[1], 0.0))
    out_even[DONOR_ROWS:, :] = even
    out_odd[DONOR_ROWS:, :] = pltpu.roll(even, LANES - CAP, 1)


def donor_kernel(fields, own, halo_odd, halo_even, after, donor_even, donor_odd, asked_out, places, sem):
    _, _, px, _ = parities()
    lane = iota((8, LANES), 1)
    even = halo_even[AT_REST:, :]
    odd = halo_odd[AT_REST:, :]
    asked = pick(
        px,
        jnp.where(lane < CAP, pltpu.roll(even, LANES - CAP, 1), pltpu.roll(odd, CAP, 1)),
        jnp.where(lane < CAP, even, odd),
    )
    asked_out[...] = asked.astype(jnp.int32)
    copy = pltpu.make_async_copy(asked_out, places, sem)
    copy.start()
    donor_offsets(own[...], asked[:1], donor_even, donor_odd)
    copy.wait()
    take_donors(fields, places, donor_even, donor_odd)


def columns_kernel(density, own, halo_odd, halo_even, y_even, y_odd, ext):
    _, _, px, py = parities()
    pack_y(density[0], halo_even, halo_odd, own[...], ext, px, py, y_even, y_odd)


def relax(fields, own, halo_even, halo_odd, y_even, y_odd, dens, ext, mon):
    tile_x, tile_y, px, py = parities()
    dens[HALO : HALO + CX, SIDE : SIDE + CY, :] = fields[0].reshape(CX, CY, NZ)
    left = pick(px, halo_even[:EDGE, :], halo_odd[:EDGE, :])
    right = pick(px, halo_odd[:EDGE, :], halo_even[:EDGE, :])
    dens[:HALO, SIDE : SIDE + CY, :] = left.reshape(HALO, CY, NZ)
    dens[HALO + CX :, SIDE : SIDE + CY, :] = right.reshape(HALO, CY, NZ)
    half = EXT // 2
    below = pick(py, y_even[:Y_DENSITY, :], y_odd[:Y_DENSITY, :]).reshape(half, 8, NZ)
    above = pick(py, y_odd[:Y_DENSITY, :], y_even[:Y_DENSITY, :]).reshape(half, 8, NZ)
    dens[:half, :SIDE, :] = pltpu.roll(below, HALO, 1)
    dens[half:, :SIDE, :] = below
    dens[:half, SIDE + CY :, :] = above
    dens[half:, SIDE + CY :, :] = pltpu.roll(above, HALO, 1)

    even = halo_even[AT_OFFSETS:AT_REST, :]
    odd = halo_odd[AT_OFFSETS:AT_REST, :]
    fill_offsets(ext, own, pick(px, even, odd), pick(px, odd, even))
    lane = iota((EXT, LANES), 1)
    half_lane = lax.rem(lane, HALF)
    even = y_even[Y_DENSITY:, :]
    odd = y_odd[Y_DENSITY:, :]
    moved = ext[...]
    moved = jnp.where(half_lane < SIDE, pltpu.roll(pick(py, even, odd), LANES - CY, 1), moved)
    moved = jnp.where(half_lane >= SIDE + CY, pltpu.roll(pick(py, odd, even), CY, 1), moved)

    spot = iota((WIDE, LANES), 0)
    diagonal = spot == lax.rem(iota((WIDE, LANES), 1), HALF)
    mon[0:1, :] = jnp.zeros((1, LANES), F32)
    mon[EXT - 1 :, :] = jnp.zeros((1, LANES), F32)
    for r in range(1, EXT - 1):
        east = dens[r + 1] - dens[r - 1]
        here = dens[r]
        north = pltpu.roll(here, WIDE - 1, 0) - pltpu.roll(here, 1, 0)
        steep = jnp.sum(east * east + north * north, axis=1, keepdims=True)
        mon[r : r + 1, :] = jnp.sum(jnp.where(diagonal, steep, 0.0), axis=0, keepdims=True)
    row_global = tile_x * CX - HALO + iota((EXT, LANES), 0)
    col_global = tile_y * CY - SIDE + half_lane
    on_grid = (row_global >= 0) & (row_global < NX) & (col_global >= 0) & (col_global < NY)
    interior = (
        (row_global >= 1) & (row_global <= NX - 2) & (col_global >= 1) & (col_global <= NY - 2)
    )
    monitor = jnp.where(on_grid, jnp.sqrt(1.0 + (BETA_COEF / NZ) * mon[...]), 0.0)

    def to_east(x):
        return pltpu.roll(x, EXT - 1, 0)

    def to_west(x):
        return pltpu.roll(x, 1, 0)

    def to_north(x):
        return pltpu.roll(x, LANES - 1, 1)

    def to_south(x):
        return pltpu.roll(x, 1, 1)

    east = monitor + to_east(monitor)
    west = monitor + to_west(monitor)
    north = monitor + to_north(monitor)
    south = monitor + to_south(monitor)
    scale = OMEGA_COEF / (east + west + north + south)
    drift = jnp.where(lane < HALF, east - west, north - south) * scale
    east = east * scale
    west = west * scale
    north = north * scale
    south = south * scale
    for _ in range(SWEEPS):
        relaxed = (
            (1.0 - OMEGA_COEF) * moved
            + east * to_east(moved)
            + west * to_west(moved)
            + north * to_north(moved)
            + south * to_south(moved)
            + drift
        )
        moved = jnp.where(interior, relaxed, moved)
    ext[...] = moved
    return ext[HALO : HALO + CX, :]


def weight(dx, dy):
    bulk = SPREAD_SQ + dx * dx + dy * dy
    guess = pl.reciprocal(bulk, approx=True)
    return guess * (2.0 - bulk * guess)


def split(x):
    high = x.astype(BF16)
    return high, (x - high.astype(F32)).astype(BF16)


def placed(shifts, r):
    along = iota((CY, 1), 0).astype(F32)
    at_x = shifts[SIDE : SIDE + CY, r : r + 1] + float(r)
    at_y = shifts[HALF + SIDE : HALF + SIDE + CY, r : r + 1] + along
    return at_x, at_y


def weigh_near(own, moved, owner, place, count, left_hand, norm):
    tile_x = lax.axis_index("gx")
    flat_x, flat_y = flat_rows(own)
    spot = iota((1, TILE), 1)
    flat_x = flat_x + (spot // CY).astype(F32)
    flat_y = flat_y + lax.rem(spot, CY).astype(F32)
    live = count[...]
    codes = []
    for k in range(DONORS):
        here = owner[:, k, :] == tile_x
        codes.append(widen(jnp.where(here & (k < live), place[:, k, :], -1).astype(F32)))
    columns = jnp.transpose(jnp.concatenate(codes, axis=0))
    shifts = jnp.transpose(moved)
    spots = iota((CY, TILE), 1).astype(F32)
    for r in range(CX):
        at_x, at_y = placed(shifts, r)
        dense = weight(at_x - flat_x, at_y - flat_y)
        total = jnp.zeros((CY, TILE), F32)
        for k in range(DONORS):
            code = columns[:CY, k * CX + r : k * CX + r + 1]
            total = total + jnp.where(code == spots, dense, 0.0)
        rows = slice(r * CY, (r + 1) * CY)
        norm[rows, :] = jnp.broadcast_to(jnp.sum(total, axis=1, keepdims=True), (CY, LANES))
        high, low = split(total)
        left_hand[rows, 0:TILE] = high
        left_hand[rows, TILE : 2 * TILE] = low
        left_hand[rows, 2 * TILE : 3 * TILE] = high


def weigh_far(moved, aux, even, odd, norm, left_hand, inverse):
    _, _, px, _ = parities()
    request = aux[CX : CX + 1, :].astype(jnp.int32)
    lane = iota((1, LANES), 1)
    left = pick(px, even, odd)
    right = pick(px, odd, even)
    far = jnp.where(iota((8, LANES), 1) < CAP, left, pltpu.roll(right, CAP, 1))
    far_x = far[0:1] + jnp.where(lane < CAP, request // CY - CX, request // CY + CX).astype(F32)
    far_y = far[1:2] + lax.rem(request, CY).astype(F32)
    far_x = jnp.where(lane < HALF, far_x, pltpu.roll(far_x, HALF, 1))
    far_y = jnp.where(lane < HALF, far_y, pltpu.roll(far_y, HALF, 1))
    far_lane = lax.rem(lane, HALF).astype(F32)
    near_half = iota((CY, LANES), 1) < HALF
    columns = jnp.transpose(aux[...])
    shifts = jnp.transpose(moved)
    for r in range(CX):
        at_x, at_y = placed(shifts, r)
        code = columns[:CY, r : r + 1]
        remote = jnp.where(code == far_lane, weight(at_x - far_x, at_y - far_y), 0.0)
        rows = slice(r * CY, (r + 1) * CY)
        total = norm[rows, :] + jnp.sum(jnp.where(near_half, remote, 0.0), axis=1, keepdims=True)
        inverse[rows, :] = 1.0 / total
        high = remote.astype(BF16).astype(F32)
        left_hand[rows, :LANES] = jnp.where(near_half, high, remote - high).astype(BF16)
        left_hand[rows, LANES:] = jnp.where(near_half, high, 0.0).astype(BF16)


def mix_near(fields, left_hand, right_hand, out):
    for f in range(FIELDS):
        n, lanes = f // 2, slice((f % 2) * NZ, (f % 2) * NZ + NZ)
        high, low = split(fields[f])
        right_hand[n, 0:TILE, lanes] = high
        right_hand[n, TILE : 2 * TILE, lanes] = high
        right_hand[n, 2 * TILE : 3 * TILE, lanes] = low
    for n in range(FIELDS // 2):
        mixed = jnp.dot(left_hand[...], right_hand[n], preferred_element_type=F32)
        out[2 * n] = mixed[:, :NZ]
        out[2 * n + 1] = mixed[:, NZ:]


def mix_far(near, even, odd, left_hand, right_hand, inverse, out, done=None):
    _, _, px, _ = parities()
    for f in range(FIELDS):
        n, lanes = f // 2, slice((f % 2) * NZ, (f % 2) * NZ + NZ)
        from_even = even[f * CAP : (f + 1) * CAP, :]
        from_odd = odd[f * CAP : (f + 1) * CAP, :]
        left, right = pick(px, from_even, from_odd), pick(px, from_odd, from_even)
        high, low = split(jnp.concatenate([left, right], axis=0))
        right_hand[n, 0:HALF, lanes] = high
        right_hand[n, HALF : 2 * HALF, lanes] = high
        right_hand[n, 2 * HALF : 3 * HALF, lanes] = low
        right_hand[n, 3 * HALF :, lanes] = jnp.zeros((HALF, NZ), BF16)
    for n in range(FIELDS // 2):
        mixed = jnp.dot(left_hand[...], right_hand[n], preferred_element_type=F32)
        out[2 * n] = (near[2 * n] + mixed[:, :NZ]) * inverse[...]
        out[2 * n + 1] = (near[2 * n + 1] + mixed[:, NZ:]) * inverse[...]
        if done is not None:
            done(n)


def near_kernel(
    fields, own, halo_odd, halo_even, y_odd, y_even, owner, place, count,
    near, moved_out, norm,
    dens, ext, mon, left_hand, right_hand,
):
    moved = relax(fields, own[...], halo_even, halo_odd, y_even, y_odd, dens, ext, mon)
    moved_out[...] = moved
    weigh_near(own[...], moved, owner, place, count, left_hand, norm)
    mix_near(fields, left_hand, right_hand, near)


def far_kernel(
    near, moved, norm, donor_odd, donor_even, aux, asked,
    out, x_even, x_odd, d_even, d_odd,
    left_hand, right_hand, inverse, places, sem,
):
    _, _, px, _ = parities()
    copy = pltpu.make_async_copy(asked, places, sem)
    copy.start()
    weigh_far(
        moved[...], aux, donor_even[DONOR_ROWS:, :], donor_odd[DONOR_ROWS:, :], norm, left_hand, inverse
    )
    mix_far(near, donor_even, donor_odd, left_hand, right_hand, inverse, out)
    low, high = out[0, :EDGE, :], out[0, TILE - EDGE :, :]
    x_even[:EDGE, :] = pick(px, low, high)
    x_odd[:EDGE, :] = pick(px, high, low)
    low, high = moved[:8, :], moved[8:, :]
    x_even[AT_OFFSETS:AT_REST, :] = pick(px, low, high)
    x_odd[AT_OFFSETS:AT_REST, :] = pick(px, high, low)
    donor_offsets(moved[...], asked[:1, :].astype(F32), d_even, d_odd)
    copy.wait()
    take_donors(out, places, d_even, d_odd)


def last_kernel(
    near, moved, norm, donor_odd, donor_even, aux,
    moved_out, out_hbm,
    left_hand, right_hand, inverse, out, sems,
):
    wide = moved[...]
    moved_out[0] = pltpu.roll(wide, LANES - SIDE, 1)[:, :CY]
    moved_out[1] = pltpu.roll(wide, HALF - SIDE, 1)[:, :CY]
    weigh_far(wide, aux, donor_even[DONOR_ROWS:, :], donor_odd[DONOR_ROWS:, :], norm, left_hand, inverse)

    def copy(n):
        pair = pl.ds(2 * n, 2)
        return pltpu.make_async_copy(out.at[pair], out_hbm.at[pair], sems.at[n])

    mix_far(
        near, donor_even, donor_odd, left_hand, right_hand, inverse, out, lambda n: copy(n).start()
    )
    for n in range(FIELDS // 2):
        copy(n).wait()


def shape(*dims, dtype=F32):
    return jax.ShapeDtypeStruct(dims, dtype)


def call(kernel, outs, scratch=(), name=None, cost=None, **extra):
    return pl.pallas_call(
        kernel,
        out_shape=outs,
        scratch_shapes=list(scratch),
        compiler_params=pltpu.CompilerParams(vmem_limit_bytes=VMEM_BYTES),
        name=name,
        cost_estimate=cost,
        **extra,
    )


def swap_pairs(block, axis, odd):
    count = lax.axis_size(axis)
    route = []
    for a in range(1 if odd else 0, count - 1, 2):
        route += [(a, a + 1), (a + 1, a)]
    return lax.ppermute(block, axis, route)


def swap(even, odd, axis):
    odd = swap_pairs(odd, axis, True)
    return swap_pairs(even, axis, False), odd


RELAX = (
    pltpu.VMEM((EXT, WIDE, NZ), F32),
    pltpu.VMEM((EXT, LANES), F32),
    pltpu.VMEM((EXT, LANES), F32),
)
NEAR = (
    pltpu.VMEM((TILE, 3 * TILE), BF16),
    pltpu.VMEM((FIELDS // 2, 3 * TILE, 2 * NZ), BF16),
)
NORM = pltpu.VMEM((TILE, LANES), F32)
FAR = (
    pltpu.VMEM((TILE, 4 * HALF), BF16),
    pltpu.VMEM((FIELDS // 2, 4 * HALF, 2 * NZ), BF16),
    NORM,
)
PLACES = (pltpu.SMEM((8, LANES), jnp.int32), pltpu.SemaphoreType.DMA)


def whole():
    return pl.BlockSpec(memory_space=pltpu.VMEM)


def columns(fields, own, halo):
    return call(
        columns_kernel,
        (shape(Y_MSG, LANES), shape(Y_MSG, LANES)),
        scratch=(pltpu.VMEM((EXT, LANES), F32),),
        grid=(1,),
        in_specs=[pl.BlockSpec((1, TILE, NZ), lambda i: (0, 0, 0)), whole(), whole(), whole()],
        name="pack_columns",
    )(fields, own, *halo[::-1])


def step_near(fields, own, halo, y_halo, owner, place, count):
    return call(
        near_kernel,
        (shape(FIELDS, TILE, NZ), shape(CX, LANES), shape(TILE, LANES)),
        scratch=RELAX + NEAR,
        name="step_near",
        cost=pl.CostEstimate(
            flops=2 * TILE * 3 * TILE * FIELDS * NZ, bytes_accessed=16 << 20, transcendentals=TILE * TILE
        ),
    )(fields, own, *halo[::-1], *y_halo[::-1], owner, place, count)


def per_device(fields, displacement, donor_tile, donor_offset, donor_count):
    fields = fields.reshape(FIELDS, TILE, NZ)
    owner = donor_tile.transpose(0, 2, 1)
    place = donor_offset.transpose(0, 2, 1)
    even, odd, own, aux = call(
        first_kernel,
        (shape(REQUEST_MSG, LANES), shape(REQUEST_MSG, LANES), shape(CX, LANES), shape(CX + 8, LANES)),
        scratch=(
            pltpu.VMEM((2, CX, CY), F32),
            pltpu.VMEM((EDGE, NZ), F32),
            pltpu.VMEM((EDGE, NZ), F32),
            pltpu.VMEM((CX, DONORS, CY), jnp.int32),
            pltpu.VMEM((CX, DONORS, CY), jnp.int32),
            pltpu.SemaphoreType.DMA((5,)),
        ),
        in_specs=[pl.BlockSpec(memory_space=pltpu.HBM)] * 4,
        name="pack_first",
    )(*(pltpu.with_memory_space_constraint(x, pltpu.HBM) for x in (displacement, fields, owner, place)))
    halo = swap(even, odd, "gx")
    y_even, y_odd = columns(fields, own, halo)
    y_halo = swap(y_even, y_odd, "gy")
    d_even, d_odd, asked = call(
        donor_kernel,
        (shape(DONOR_MSG, LANES), shape(DONOR_MSG, LANES), shape(8, LANES, dtype=jnp.int32)),
        scratch=PLACES,
        name="pack_donors",
    )(fields, own, *halo[::-1], y_even)
    donors = swap(d_even, d_odd, "gx")
    near, own, norm = step_near(fields, own, halo, y_halo, owner, place, donor_count)
    fields, even, odd, d_even, d_odd = call(
        far_kernel,
        (
            shape(FIELDS, TILE, NZ), shape(AT_REST, LANES), shape(AT_REST, LANES),
            shape(DONOR_MSG, LANES), shape(DONOR_MSG, LANES),
        ),
        scratch=FAR + PLACES,
        name="step_one_far",
    )(near, own, norm, *donors[::-1], aux, asked)
    halo = swap(even, odd, "gx")
    y_halo = swap(*columns(fields, own, halo), "gy")
    donors = swap(d_even, d_odd, "gx")
    near, own, norm = step_near(fields, own, halo, y_halo, owner, place, donor_count)
    moved, fields = call(
        last_kernel,
        (shape(2, CX, CY), shape(FIELDS, TILE, NZ)),
        scratch=FAR + (pltpu.VMEM((FIELDS, TILE, NZ), F32), pltpu.SemaphoreType.DMA((FIELDS // 2,))),
        out_specs=(whole(), pl.BlockSpec(memory_space=pltpu.HBM)),
        name="step_two_far",
    )(near, own, norm, *donors[::-1], aux)
    return moved, fields.reshape(FIELDS, CX, CY, NZ)


def solution(mesh):
    return jax.shard_map(
        per_device,
        mesh=mesh,
        in_specs=(
            P(None, "gx", "gy", None),
            P(None, "gx", "gy"),
            P("gx", "gy", None),
            P("gx", "gy", None),
            P("gx", "gy"),
        ),
        out_specs=(P(None, "gx", "gy"), P(None, "gx", "gy", None)),
        check_vma=False,
    )
```

```python
import jax
import jax.numpy as jnp
from jax import lax
from jax.experimental import pallas as pl
from jax.experimental.pallas import tpu as pltpu
from jax.sharding import PartitionSpec as P

CX = 16
CY = 32
NZ = 128
FIELDS = 8
DONORS = 4
CAP = 32
SWEEPS = 3
STEPS = 2
NX = 512
NY = 512

BETA_COEF = 0.5
OMEGA_COEF = 0.6
SPREAD_SQ = 64.0

TILE = CX * CY
HALO = 4
EXT = CX + 2 * HALO
SIDE = 8
WIDE = CY + 2 * SIDE
HALF = 64
LANES = 128
EDGE = HALO * CY
AT_OFFSETS = EDGE
AT_REST = EDGE + 8
DONOR_ROWS = FIELDS * CAP
REQUEST_MSG = AT_REST + 8
DONOR_MSG = DONOR_ROWS + 8
Y_DENSITY = EXT * HALO
Y_MSG = Y_DENSITY + EXT

F32 = jnp.float32
BF16 = jnp.bfloat16
VMEM_BYTES = 20 * 1024 * 1024


def iota(shape, dim):
    return lax.broadcasted_iota(jnp.int32, shape, dim)


def pick(flag, a, b):
    return jnp.where(jnp.full(a.shape, flag, jnp.int32) != 0, a, b)


def widen(x):
    return jnp.concatenate([x, jnp.zeros((x.shape[0], LANES - x.shape[1]), x.dtype)], axis=1)


def spread(x, y):
    gap = jnp.zeros((CX, CY), F32)
    return pltpu.roll(jnp.concatenate([x, gap, y, gap], axis=1), SIDE, 1)


def parities():
    tile_x = lax.axis_index("gx")
    tile_y = lax.axis_index("gy")
    return tile_x, tile_y, lax.rem(tile_x, 2), lax.rem(tile_y, 2)


def first_kernel(
    disp_hbm, fields_hbm, owner_hbm, place_hbm, out_even, out_odd, own, aux, slots, disp, head, tail, owner, place, sems
):
    tile_x, _, px, _ = parities()
    copies = [
        pltpu.make_async_copy(source, target, sems.at[i])
        for i, (source, target) in enumerate(
            (
                (owner_hbm, owner),
                (place_hbm, place),
                (disp_hbm, disp),
                (fields_hbm.at[0, pl.ds(0, EDGE)], head),
                (fields_hbm.at[0, pl.ds(TILE - EDGE, EDGE)], tail),
            )
        )
    ]
    for copy in copies:
        copy.start()
    for copy in copies:
        copy.wait()
    offsets = spread(disp[0], disp[1])
    own[...] = offsets
    first_owner = owner[:, 0, :]
    to_left = widen((first_owner == tile_x - 1).astype(F32))
    to_right = widen((first_owner == tile_x + 1).astype(F32))
    marks = jnp.concatenate([to_left, to_right], axis=0)
    earlier = (iota((LANES, LANES), 0) < iota((LANES, LANES), 1)).astype(F32)
    in_row = jnp.dot(marks, earlier, preferred_element_type=F32)
    totals = jnp.broadcast_to(jnp.sum(marks, axis=1, keepdims=True), (2 * CX, LANES))
    row = lax.rem(iota((2 * CX, LANES), 0), CX)
    before = totals
    for step in (1, 2, 4, 8):
        before = before + jnp.where(row >= step, pltpu.roll(before, step, 0), 0.0)
    rank = in_row + before - totals
    code = jnp.where(
        to_left > 0, rank[:CX], jnp.where(to_right > 0, rank[CX:] + CAP, -1.0)
    )
    columns = jnp.transpose(jnp.concatenate([code, widen(place[:, 0, :].astype(F32))], axis=0))
    lane = iota((CY, LANES), 1).astype(F32)
    spot = iota((CY, LANES), 0).astype(F32)
    asked = jnp.zeros((CY, LANES), F32)
    used = jnp.zeros((CY, LANES), F32)
    for r in range(CX):
        hit = columns[:CY, r : r + 1] == lane
        asked = asked + jnp.where(hit, columns[:CY, CX + r : CX + r + 1], 0.0)
        used = used + jnp.where(hit, spot + float(r * CY + 1), 0.0)
    request = jnp.broadcast_to(jnp.sum(asked, axis=0, keepdims=True), (8, LANES))
    aux[...] = request
    used = jnp.broadcast_to(jnp.sum(used, axis=0, keepdims=True), (8, LANES)).astype(jnp.int32)
    slots[...] = jnp.where(used > 0, used - 1, TILE)
    low, high = head[...], tail[...]
    out_even[:EDGE, :] = pick(px, low, high)
    out_odd[:EDGE, :] = pick(px, high, low)
    low, high = offsets[:8], offsets[8:]
    out_even[AT_OFFSETS:AT_REST, :] = pick(px, low, high)
    out_odd[AT_OFFSETS:AT_REST, :] = pick(px, high, low)
    out_even[AT_REST:, :] = request
    out_odd[AT_REST:, :] = request


def fill_offsets(ext, own, left, right):
    ext[0:HALO, :] = left[HALO:8]
    ext[HALO : HALO + CX, :] = own
    ext[HALO + CX :, :] = right[0:HALO]


def edge_columns(density, from_left, from_right, start):
    parts = []
    for part, rows in ((from_left, HALO), (density, CX), (from_right, HALO)):
        parts.append(part.reshape(rows, CY, NZ)[:, start : start + 8, :])
    return jnp.concatenate(parts, axis=0)


def pack_y(density, halo_even, halo_odd, own, ext, px, py, out_even, out_odd):
    from_left = pick(px, halo_even[:EDGE, :], halo_odd[:EDGE, :])
    from_right = pick(px, halo_odd[:EDGE, :], halo_even[:EDGE, :])
    even = halo_even[AT_OFFSETS:AT_REST, :]
    odd = halo_odd[AT_OFFSETS:AT_REST, :]
    fill_offsets(ext, own, pick(px, even, odd), pick(px, odd, even))
    half = EXT // 2
    low = edge_columns(density, from_left, from_right, 0)
    high = edge_columns(density, from_left, from_right, CY - 8)
    sub = iota((half, 8, NZ), 1)
    low = jnp.where(sub < HALO, low[:half], pltpu.roll(low[half:], HALO, 1))
    high = jnp.where(sub < HALO, pltpu.roll(high[:half], HALO, 1), high[half:])
    low = low.reshape(Y_DENSITY, NZ)
    high = high.reshape(Y_DENSITY, NZ)
    out_even[:Y_DENSITY, :] = pick(py, low, high)
    out_odd[:Y_DENSITY, :] = pick(py, high, low)
    out_even[Y_DENSITY:, :] = ext[...]
    out_odd[Y_DENSITY:, :] = ext[...]


def take_donors(fields, places, out_even, out_odd):
    def one(r, carry):
        for out, shift in ((out_even, 0), (out_odd, CAP)):
            p = places[0, r + shift]
            for f in range(FIELDS):
                out[pl.ds(f * CAP + r, 1), :] = fields[f, pl.ds(p, 1), :]
        return carry

    lax.fori_loop(0, CAP, one, 0, unroll=8)


def flat_rows(wide):
    row = iota((CX, LANES), 0)
    lane = iota((CX, LANES), 1)
    outs = []
    for base in (SIDE, HALF + SIDE):
        pieces = jnp.zeros((CX, LANES), F32)
        for m in range(4):
            moved = pltpu.roll(wide, (m * CY - base) % LANES, 1)
            pieces = pieces + jnp.where((row % 4 == m) & (lane // CY == m), moved, 0.0)
        quarters = [
            jnp.sum(jnp.where(row // 4 == q, pieces, 0.0), axis=0, keepdims=True) for q in range(4)
        ]
        outs.append(jnp.concatenate(quarters, axis=1))
    return outs


def at_columns(flats, wanted):
    sub = iota((HALF, LANES), 0)
    lane = iota((HALF, LANES), 1)
    column = jnp.sum(
        jnp.where(sub == lane, jnp.broadcast_to(wanted, (HALF, LANES)), 0.0), axis=1, keepdims=True
    )
    hit = column == iota((HALF, TILE), 1).astype(F32)
    return [jnp.sum(jnp.where(hit, flat, 0.0), axis=1, keepdims=True) for flat in flats]


def offset_rows(flats, wanted):
    diagonal = iota((HALF, LANES), 0) == iota((HALF, LANES), 1)
    rows = [
        jnp.sum(jnp.where(diagonal, column, 0.0), axis=0, keepdims=True)
        for column in at_columns(flats, wanted)
    ]
    place = iota((8, LANES), 0)
    return jnp.where(place == 0, rows[0], jnp.where(place == 1, rows[1], 0.0))


def donor_kernel(fields, own, halo_odd, halo_even, donor_even, donor_odd, asked_out, places, sem):
    _, _, px, _ = parities()
    lane = iota((8, LANES), 1)
    even = halo_even[AT_REST:, :]
    odd = halo_odd[AT_REST:, :]
    asked = pick(
        px,
        jnp.where(lane < CAP, pltpu.roll(even, LANES - CAP, 1), pltpu.roll(odd, CAP, 1)),
        jnp.where(lane < CAP, even, odd),
    )
    asked_out[...] = asked.astype(jnp.int32)
    copy = pltpu.make_async_copy(asked_out, places, sem)
    copy.start()
    offsets = offset_rows(flat_rows(own[...]), asked[:1])
    donor_even[DONOR_ROWS:, :] = offsets
    donor_odd[DONOR_ROWS:, :] = pltpu.roll(offsets, LANES - CAP, 1)
    copy.wait()
    take_donors(fields, places, donor_even, donor_odd)


def columns_kernel(density, own, halo_odd, halo_even, y_even, y_odd, ext):
    _, _, px, py = parities()
    pack_y(density[0], halo_even, halo_odd, own[...], ext, px, py, y_even, y_odd)


def relax(fields, own, halo_even, halo_odd, y_even, y_odd, dens, ext, mon):
    tile_x, tile_y, px, py = parities()
    dens[HALO : HALO + CX, SIDE : SIDE + CY, :] = fields[0, :TILE, :].reshape(CX, CY, NZ)
    left = pick(px, halo_even[:EDGE, :], halo_odd[:EDGE, :])
    right = pick(px, halo_odd[:EDGE, :], halo_even[:EDGE, :])
    dens[:HALO, SIDE : SIDE + CY, :] = left.reshape(HALO, CY, NZ)
    dens[HALO + CX :, SIDE : SIDE + CY, :] = right.reshape(HALO, CY, NZ)
    half = EXT // 2
    below = pick(py, y_even[:Y_DENSITY, :], y_odd[:Y_DENSITY, :]).reshape(half, 8, NZ)
    above = pick(py, y_odd[:Y_DENSITY, :], y_even[:Y_DENSITY, :]).reshape(half, 8, NZ)
    dens[:half, :SIDE, :] = pltpu.roll(below, HALO, 1)
    dens[half:, :SIDE, :] = below
    dens[:half, SIDE + CY :, :] = above
    dens[half:, SIDE + CY :, :] = pltpu.roll(above, HALO, 1)

    even = halo_even[AT_OFFSETS:AT_REST, :]
    odd = halo_odd[AT_OFFSETS:AT_REST, :]
    fill_offsets(ext, own, pick(px, even, odd), pick(px, odd, even))
    lane = iota((EXT, LANES), 1)
    half_lane = lax.rem(lane, HALF)
    even = y_even[Y_DENSITY:, :]
    odd = y_odd[Y_DENSITY:, :]
    moved = ext[...]
    moved = jnp.where(half_lane < SIDE, pltpu.roll(pick(py, even, odd), LANES - CY, 1), moved)
    moved = jnp.where(half_lane >= SIDE + CY, pltpu.roll(pick(py, odd, even), CY, 1), moved)

    spot = iota((WIDE, LANES), 0)
    diagonal = spot == lax.rem(iota((WIDE, LANES), 1), HALF)
    mon[0:1, :] = jnp.zeros((1, LANES), F32)
    mon[EXT - 1 :, :] = jnp.zeros((1, LANES), F32)
    for r in range(1, EXT - 1):
        east = dens[r + 1] - dens[r - 1]
        here = dens[r]
        north = pltpu.roll(here, WIDE - 1, 0) - pltpu.roll(here, 1, 0)
        steep = jnp.sum(east * east + north * north, axis=1, keepdims=True)
        mon[r : r + 1, :] = jnp.sum(jnp.where(diagonal, steep, 0.0), axis=0, keepdims=True)
    row_global = tile_x * CX - HALO + iota((EXT, LANES), 0)
    col_global = tile_y * CY - SIDE + half_lane
    on_grid = (row_global >= 0) & (row_global < NX) & (col_global >= 0) & (col_global < NY)
    interior = (
        (row_global >= 1) & (row_global <= NX - 2) & (col_global >= 1) & (col_global <= NY - 2)
    )
    monitor = jnp.where(on_grid, jnp.sqrt(1.0 + (BETA_COEF / NZ) * mon[...]), 0.0)

    def to_east(x):
        return pltpu.roll(x, EXT - 1, 0)

    def to_west(x):
        return pltpu.roll(x, 1, 0)

    def to_north(x):
        return pltpu.roll(x, LANES - 1, 1)

    def to_south(x):
        return pltpu.roll(x, 1, 1)

    east = monitor + to_east(monitor)
    west = monitor + to_west(monitor)
    north = monitor + to_north(monitor)
    south = monitor + to_south(monitor)
    scale = OMEGA_COEF / (east + west + north + south)
    drift = jnp.where(lane < HALF, east - west, north - south) * scale
    east = east * scale
    west = west * scale
    north = north * scale
    south = south * scale
    for _ in range(SWEEPS):
        relaxed = (
            (1.0 - OMEGA_COEF) * moved
            + east * to_east(moved)
            + west * to_west(moved)
            + north * to_north(moved)
            + south * to_south(moved)
            + drift
        )
        moved = jnp.where(interior, relaxed, moved)
    ext[...] = moved
    return ext[HALO : HALO + CX, :]


def weight(dx, dy):
    bulk = SPREAD_SQ + dx * dx + dy * dy
    guess = pl.reciprocal(bulk, approx=True)
    return guess * (2.0 - bulk * guess)


def split(x):
    high = x.astype(BF16)
    return high, (x - high.astype(F32)).astype(BF16)


def placed(shifts, r):
    along = iota((CY, 1), 0).astype(F32)
    at_x = shifts[SIDE : SIDE + CY, r : r + 1] + float(r)
    at_y = shifts[HALF + SIDE : HALF + SIDE + CY, r : r + 1] + along
    return at_x, at_y


def weigh_near(own, moved, owner, place, count, left_hand, norm, inverse):
    tile_x = lax.axis_index("gx")
    flat_x, flat_y = flat_rows(own)
    spot = iota((1, TILE), 1)
    flat_x = flat_x + (spot // CY).astype(F32)
    flat_y = flat_y + lax.rem(spot, CY).astype(F32)
    live = count[...]
    codes = []
    for k in range(DONORS):
        here = owner[:, k, :] == tile_x
        codes.append(widen(jnp.where(here & (k < live), place[:, k, :], -1).astype(F32)))
    columns = jnp.transpose(jnp.concatenate(codes, axis=0))
    shifts = jnp.transpose(moved)
    spots = iota((CY, TILE), 1).astype(F32)
    for r in range(CX):
        at_x, at_y = placed(shifts, r)
        dense = weight(at_x - flat_x, at_y - flat_y)
        total = jnp.zeros((CY, TILE), F32)
        for k in range(DONORS):
            code = columns[:CY, k * CX + r : k * CX + r + 1]
            total = total + jnp.where(code == spots, dense, 0.0)
        rows = slice(r * CY, (r + 1) * CY)
        sums = jnp.broadcast_to(jnp.sum(total, axis=1, keepdims=True), (CY, LANES))
        norm[rows, :] = sums
        inverse[rows, :] = jnp.where(sums > 0, 1.0 / sums, 0.0)
        high, low = split(total)
        left_hand[rows, 0:TILE] = high
        left_hand[rows, TILE : 2 * TILE] = low
        left_hand[rows, 2 * TILE : 3 * TILE] = high


def mix_near(fields, left_hand, right_hand, inverse, out):
    for f in range(FIELDS):
        n, lanes = f // 2, slice((f % 2) * NZ, (f % 2) * NZ + NZ)
        high, low = split(fields[f, :TILE, :])
        right_hand[n, 0:TILE, lanes] = high
        right_hand[n, TILE : 2 * TILE, lanes] = high
        right_hand[n, 2 * TILE : 3 * TILE, lanes] = low
    for n in range(FIELDS // 2):
        mixed = jnp.dot(left_hand[...], right_hand[n], preferred_element_type=F32)
        out[2 * n, :TILE, :] = mixed[:, :NZ] * inverse[...]
        out[2 * n + 1, :TILE, :] = mixed[:, NZ:] * inverse[...]


def near_body(
    fields, own, halo_odd, halo_even, y_odd, y_even, owner, place, count, slots, asked,
    near, moved_out, ranked, ranked_norm, ranked_at, next_offsets,
    dens, ext, mon, left_hand, right_hand, norm, inverse, seats, sem,
):
    copy = pltpu.make_async_copy(slots, seats, sem)
    copy.start()
    moved = relax(fields, own[...], halo_even, halo_odd, y_even, y_odd, dens, ext, mon)
    moved_out[...] = moved
    flats = flat_rows(moved)
    if asked is not None:
        next_offsets[...] = offset_rows(flats, asked[:1, :].astype(F32))
    spot = iota((1, TILE), 1)
    flats = [flats[0] + (spot // CY).astype(F32), flats[1] + lax.rem(spot, CY).astype(F32)]
    at_x, at_y = at_columns(flats, slots[:1, :].astype(F32))
    ranked_at[0] = jnp.broadcast_to(at_x, (HALF, LANES))
    ranked_at[1] = jnp.broadcast_to(at_y, (HALF, LANES))
    weigh_near(own[...], moved, owner, place, count, left_hand, norm, inverse)
    norm[TILE:, :] = jnp.zeros((8, LANES), F32)
    near[:, TILE:, :] = jnp.zeros((FIELDS, 8, NZ), F32)
    mix_near(fields, left_hand, right_hand, inverse, near)
    copy.wait()

    def one(r, carry):
        seat = seats[0, r]
        ranked_norm[pl.ds(r, 1), :] = norm[pl.ds(seat, 1), :]
        for f in range(FIELDS):
            ranked[f, pl.ds(r, 1), :] = near[f, pl.ds(seat, 1), :]
        return carry

    lax.fori_loop(0, 2 * CAP, one, 0, unroll=8)


def near_kernel_one(*refs):
    near_body(*refs)


def near_kernel_two(*refs):
    near_body(*refs[:10], None, *refs[10:15], None, *refs[15:])


def far_weights(aux, donor_even, donor_odd, ranked_norm, ranked_at):
    _, _, px, _ = parities()
    even, odd = donor_even[DONOR_ROWS:, :], donor_odd[DONOR_ROWS:, :]
    request = aux[:1, :].astype(jnp.int32)
    lane = iota((1, LANES), 1)
    left = pick(px, even, odd)
    right = pick(px, odd, even)
    far = jnp.where(iota((8, LANES), 1) < CAP, left, pltpu.roll(right, CAP, 1))
    far_x = far[0:1] + jnp.where(lane < CAP, request // CY - CX, request // CY + CX).astype(F32)
    far_y = far[1:2] + lax.rem(request, CY).astype(F32)
    diagonal = iota((HALF, LANES), 0) == iota((HALF, LANES), 1)
    far_x = jnp.sum(jnp.where(diagonal, far_x, 0.0), axis=1, keepdims=True)
    far_y = jnp.sum(jnp.where(diagonal, far_y, 0.0), axis=1, keepdims=True)
    far_weight = weight(ranked_at[0] - far_x, ranked_at[1] - far_y)
    norm = ranked_norm[...]
    inverse = 1.0 / (norm + far_weight)
    return norm * inverse, far_weight * inverse


def patch(f, near, ranked, shares, donor_even, donor_odd, px, seats, fresh, out):
    rows = slice(f * CAP, (f + 1) * CAP)
    even, odd = donor_even[rows, :], donor_odd[rows, :]
    far = jnp.concatenate([pick(px, even, odd), pick(px, odd, even)], axis=0)
    fresh[f] = shares[0] * ranked[f] + shares[1] * far
    out[f] = near[f]

    def one(r, carry):
        out[f, pl.ds(seats[0, r], 1), :] = fresh[f, pl.ds(r, 1), :]
        return carry

    lax.fori_loop(0, 2 * CAP, one, 0, unroll=16)


def far_kernel(
    near, moved, ranked, ranked_norm, ranked_at, donor_odd, donor_even, aux, slots,
    out, x_even, x_odd,
    fresh, seats, sem,
):
    _, _, px, _ = parities()
    copy = pltpu.make_async_copy(slots, seats, sem)
    copy.start()
    shares = far_weights(aux, donor_even, donor_odd, ranked_norm, ranked_at)
    copy.wait()
    for f in range(FIELDS):
        patch(f, near, ranked, shares, donor_even, donor_odd, px, seats, fresh, out)
    low, high = out[0, :EDGE, :], out[0, TILE - EDGE : TILE, :]
    x_even[:EDGE, :] = pick(px, low, high)
    x_odd[:EDGE, :] = pick(px, high, low)
    low, high = moved[:8, :], moved[8:, :]
    x_even[AT_OFFSETS:AT_REST, :] = pick(px, low, high)
    x_odd[AT_OFFSETS:AT_REST, :] = pick(px, high, low)


def next_donor_kernel(fields, asked, next_offsets, after_odd, after_even, d_even, d_odd, places, sem):
    copy = pltpu.make_async_copy(asked, places, sem)
    copy.start()
    offsets = next_offsets[...]
    d_even[DONOR_ROWS:, :] = offsets
    d_odd[DONOR_ROWS:, :] = pltpu.roll(offsets, LANES - CAP, 1)
    copy.wait()
    take_donors(fields, places, d_even, d_odd)


def last_kernel(
    near, moved, ranked, ranked_norm, ranked_at, donor_odd, donor_even, aux, slots,
    moved_out, out_hbm,
    fresh, seats, out, sem, sems,
):
    _, _, px, _ = parities()
    copy = pltpu.make_async_copy(slots, seats, sem)
    copy.start()
    wide = moved[...]
    moved_out[0] = pltpu.roll(wide, LANES - SIDE, 1)[:, :CY]
    moved_out[1] = pltpu.roll(wide, HALF - SIDE, 1)[:, :CY]
    shares = far_weights(aux, donor_even, donor_odd, ranked_norm, ranked_at)
    copy.wait()

    def send(f):
        return pltpu.make_async_copy(out.at[f, pl.ds(0, TILE)], out_hbm.at[f], sems.at[f])

    for f in range(FIELDS):
        patch(f, near, ranked, shares, donor_even, donor_odd, px, seats, fresh, out)
        send(f).start()
    for f in range(FIELDS):
        send(f).wait()


def shape(*dims, dtype=F32):
    return jax.ShapeDtypeStruct(dims, dtype)


def call(kernel, outs, scratch=(), name=None, cost=None, **extra):
    return pl.pallas_call(
        kernel,
        out_shape=outs,
        scratch_shapes=list(scratch),
        compiler_params=pltpu.CompilerParams(vmem_limit_bytes=VMEM_BYTES),
        name=name,
        cost_estimate=cost,
        **extra,
    )


def swap_pairs(block, axis, odd):
    count = lax.axis_size(axis)
    route = []
    for a in range(1 if odd else 0, count - 1, 2):
        route += [(a, a + 1), (a + 1, a)]
    return lax.ppermute(block, axis, route)


def swap(even, odd, axis):
    odd = swap_pairs(odd, axis, True)
    return swap_pairs(even, axis, False), odd


RELAX = (
    pltpu.VMEM((EXT, WIDE, NZ), F32),
    pltpu.VMEM((EXT, LANES), F32),
    pltpu.VMEM((EXT, LANES), F32),
)
NEAR = (
    pltpu.VMEM((TILE, 3 * TILE), BF16),
    pltpu.VMEM((FIELDS // 2, 3 * TILE, 2 * NZ), BF16),
)
PADDED = TILE + 8
NORMS = (pltpu.VMEM((PADDED, LANES), F32), pltpu.VMEM((TILE, LANES), F32))
SEATS = pltpu.SMEM((8, LANES), jnp.int32)
PLACES = (SEATS, pltpu.SemaphoreType.DMA)
FRESH = pltpu.VMEM((FIELDS, HALF, NZ), F32)


def whole():
    return pl.BlockSpec(memory_space=pltpu.VMEM)


def columns(fields, own, halo):
    return call(
        columns_kernel,
        (shape(Y_MSG, LANES), shape(Y_MSG, LANES)),
        scratch=(pltpu.VMEM((EXT, LANES), F32),),
        grid=(1,),
        in_specs=[pl.BlockSpec((1, TILE, NZ), lambda i: (0, 0, 0)), whole(), whole(), whole()],
        name="pack_columns",
    )(fields, own, *halo[::-1])


def step_near(kernel, *args):
    outs = (
        shape(FIELDS, PADDED, NZ), shape(CX, LANES), shape(FIELDS, HALF, NZ), shape(HALF, LANES),
        shape(2, HALF, LANES), shape(8, LANES),
    )
    return call(
        kernel,
        outs if kernel is near_kernel_one else outs[:5],
        scratch=RELAX + NEAR + NORMS + PLACES,
        name="step_near",
        cost=None if kernel is near_kernel_two else pl.CostEstimate(
            flops=2 * TILE * 3 * TILE * FIELDS * NZ, bytes_accessed=16 << 20, transcendentals=TILE * TILE
        ),
    )(*args)


def per_device(fields, displacement, donor_tile, donor_offset, donor_count):
    fields = fields.reshape(FIELDS, TILE, NZ)
    owner = donor_tile.transpose(0, 2, 1)
    place = donor_offset.transpose(0, 2, 1)
    even, odd, own, aux, slots = call(
        first_kernel,
        (shape(REQUEST_MSG, LANES), shape(REQUEST_MSG, LANES), shape(CX, LANES), shape(8, LANES),
         shape(8, LANES, dtype=jnp.int32)),
        scratch=(
            pltpu.VMEM((2, CX, CY), F32),
            pltpu.VMEM((EDGE, NZ), F32),
            pltpu.VMEM((EDGE, NZ), F32),
            pltpu.VMEM((CX, DONORS, CY), jnp.int32),
            pltpu.VMEM((CX, DONORS, CY), jnp.int32),
            pltpu.SemaphoreType.DMA((5,)),
        ),
        in_specs=[pl.BlockSpec(memory_space=pltpu.HBM)] * 4,
        name="pack_first",
    )(*(pltpu.with_memory_space_constraint(x, pltpu.HBM) for x in (displacement, fields, owner, place)))
    halo = swap(even, odd, "gx")
    y_even, y_odd = columns(fields, own, halo)
    y_halo = swap(y_even, y_odd, "gy")
    d_even, d_odd, asked = call(
        donor_kernel,
        (shape(DONOR_MSG, LANES), shape(DONOR_MSG, LANES), shape(8, LANES, dtype=jnp.int32)),
        scratch=PLACES,
        name="pack_donors",
    )(fields, own, *halo[::-1])
    donors = swap(d_even, d_odd, "gx")
    plan = (owner, place, donor_count, slots)
    near, own, ranked, norm, at, offsets = step_near(
        near_kernel_one, fields, own, *halo[::-1], *y_halo[::-1], *plan, asked
    )
    fields, even, odd = call(
        far_kernel,
        (shape(FIELDS, PADDED, NZ), shape(AT_REST, LANES), shape(AT_REST, LANES)),
        scratch=(FRESH,) + PLACES,
        name="step_one_far",
    )(near, own, ranked, norm, at, *donors[::-1], aux, slots)
    halo = swap(even, odd, "gx")
    donors = swap(
        *call(
            next_donor_kernel,
            (shape(DONOR_MSG, LANES), shape(DONOR_MSG, LANES)),
            scratch=PLACES,
            name="pack_next_donors",
        )(fields, asked, offsets, *halo[::-1]),
        "gx",
    )
    y_halo = swap(*columns(fields, own, halo), "gy")
    near, own, ranked, norm, at = step_near(
        near_kernel_two, fields, own, *halo[::-1], *y_halo[::-1], *plan
    )
    moved, fields = call(
        last_kernel,
        (shape(2, CX, CY), shape(FIELDS, TILE, NZ)),
        scratch=(
            FRESH, SEATS, pltpu.VMEM((FIELDS, PADDED, NZ), F32),
            pltpu.SemaphoreType.DMA, pltpu.SemaphoreType.DMA((FIELDS,)),
        ),
        out_specs=(whole(), pl.BlockSpec(memory_space=pltpu.HBM)),
        name="step_two_far",
    )(near, own, ranked, norm, at, *donors[::-1], aux, slots)
    return moved, fields.reshape(FIELDS, CX, CY, NZ)


def solution(mesh):
    return jax.shard_map(
        per_device,
        mesh=mesh,
        in_specs=(
            P(None, "gx", "gy", None),
            P(None, "gx", "gy"),
            P("gx", "gy", None),
            P("gx", "gy", None),
            P("gx", "gy"),
        ),
        out_specs=(P(None, "gx", "gy"), P(None, "gx", "gy", None)),
        check_vma=False,
    )
```
